32 devices in a mesh: gx: 4 (over y, core), gy: 8 (over z, x).
Axes of the slice: x: 2, y: 2, z: 4, core: 2. Of those that a mesh axis runs over, the one named last changes fastest.
Arguments:
- features: bfloat16 [4096, 128], P(('gx', 'gy'))
- positions: float32 [3, 4096], P(None, ('gx', 'gy')), as said below
- wave_vectors: int32 [3, 16384], replicated, may hold values from -24 to 24, as said below
- filter_width: float32 [16], replicated, may hold values from 0.002 to 0.02
- w_charge: bfloat16 [128, 16], replicated, may hold values from -0.5 to 0.5
- w_filter_in: bfloat16 [20, 128], replicated, may hold values from -1.25 to 1.25
- filter_output_weight: bfloat16 [128, 128], replicated, may hold values from -0.5 to 0.5
- update_weight: bfloat16 [128, 128], replicated, may hold values from -0.125 to 0.125
- w_long: float32 [16, 128], replicated, may hold values from -1.5 to 1.5
- send_along_x: int32 [2, 1024], P(None, ('gx', 'gy')), may hold values from 0 to 127, as said below
- send_along_y: int32 [2, 1024], P(None, ('gx', 'gy')), may hold values from 0 to 191, as said below
- neighbours: int32 [64, 4096], P(None, ('gx', 'gy')), may hold values from 0 to 255
- neighbour_count: int32 [4096], P(('gx', 'gy')), may hold values from 8 to 64, as said below
- distances: float32 [64, 4096], P(None, ('gx', 'gy')), may hold values from 0.8 to 4.8
Outputs:
- updated: bfloat16 [4096, 128], P(('gx', 'gy'))
- forces: float32 [3, 4096], P(None, ('gx', 'gy'))
The draws below stay inside these ranges and needn't reach their ends.
Inputs may be any that keep to these rules, and one draw needn't show every extreme that they name: `positions`: fractional coordinates; atom i lies inside the x-y cell of its domain, z below one half. `wave_vectors`: distinct integer triples with a first component of 1 to 24 and the others from -24 to 23. `send_along_x`: each list of a domain holds 32 distinct atoms of that domain. `send_along_y`: each list of a domain holds 32 distinct rows of that domain's first_table. `neighbours`: rows of the ghost table of the atom's domain; slots at or past neighbour_count are unused. `neighbour_count`: every domain has an atom with all 64 slots used.
All inputs are finite; a program needn't handle non-finite values.
Results may differ from the reference program's by a relative error of at most 0.0062.
Values may be sent and summed in bfloat16 or wider, within the bound.
No kernel may reach another device: no remote copies, remote signals or barrier semaphores. Data moves between devices by JAX's collectives and lax.ppermute only.
A program may use at most 128 MiB of HBM per device.

```python
import math
import jax
import jax.numpy as jnp
from jax import lax

FEATURE_WIDTH = 128
C = 16
K = 16384
NRBF = 20
NEIGHBOUR_SLOTS = 64
DOMAIN_ATOMS = 128
GHOST_ROWS = 32
TOTAL_ATOMS = 4096
N_GX = 4
N_GY = 8


def draw_features(key, part):
    key = jax.random.fold_in(key, 1)
    key_spread, key_base, key_offset = jax.random.split(key, 3)
    ranking = jnp.arange(TOTAL_ATOMS, dtype=jnp.float32) / TOTAL_ATOMS
    spread = jax.random.uniform(key_spread, (TOTAL_ATOMS,), jnp.float32)
    scaling = 0.1 * jnp.exp(math.log(3.0) * ranking) * jnp.exp(math.log(10.0) * spread)
    base = jax.random.normal(key_base, (TOTAL_ATOMS, FEATURE_WIDTH), jnp.float32)
    offset = jax.random.uniform(key_offset, (FEATURE_WIDTH,), jnp.float32, -1.0, 1.0)
    return (scaling[:, None] * (base + offset[None, :])).astype(jnp.bfloat16)


def draw_positions(key, part):
    key = jax.random.fold_in(key, 2)
    key_x, key_y, key_z = jax.random.split(key, 3)
    domain = jnp.arange(TOTAL_ATOMS, dtype=jnp.int32) // DOMAIN_ATOMS
    cell_x = (domain // N_GY).astype(jnp.float32)
    cell_y = (domain % N_GY).astype(jnp.float32)
    along_x = (cell_x + jax.random.uniform(key_x, (TOTAL_ATOMS,), jnp.float32)) / N_GX
    along_y = (cell_y + jax.random.uniform(key_y, (TOTAL_ATOMS,), jnp.float32)) / N_GY
    height = jax.random.uniform(key_z, (TOTAL_ATOMS,), jnp.float32)
    along_z = 0.5 * height
    return jnp.stack([along_x, along_y, along_z]).astype(jnp.float32)


def draw_wave_vectors(key, part):
    key = jax.random.fold_in(key, 3)
    chosen = jax.random.permutation(key, 24 * 48 * 48)[:K].astype(jnp.int32)
    first = chosen // 2304 + 1
    rest = chosen % 2304
    second = rest // 48 - 24
    third = rest % 48 - 24
    return jnp.stack([first, second, third]).astype(jnp.int32)


def draw_lists(key, limit):
    block_list = TOTAL_ATOMS // DOMAIN_ATOMS
    keys = jax.random.split(key, 2 * block_list)
    chosen = jax.vmap(lambda single: jax.random.permutation(single, limit)[:GHOST_ROWS])(keys)
    return chosen.reshape(2, block_list * GHOST_ROWS).astype(jnp.int32)


def draw_send_along_x(key, part):
    key = jax.random.fold_in(key, 5)
    return draw_lists(key, DOMAIN_ATOMS)


def draw_send_along_y(key, part):
    key = jax.random.fold_in(key, 6)
    return draw_lists(key, DOMAIN_ATOMS + 2 * GHOST_ROWS)


def draw_neighbour_count(key, part):
    key = jax.random.fold_in(key, 4)
    key_total_count, key_pick = jax.random.split(key, 2)
    block_list = TOTAL_ATOMS // DOMAIN_ATOMS
    count_values = jax.random.randint(key_total_count, (block_list, DOMAIN_ATOMS), NEIGHBOUR_SLOTS // 8, NEIGHBOUR_SLOTS + 1)
    picked_rows = jax.random.randint(key_pick, (block_list, 1), 0, DOMAIN_ATOMS)
    count_values = jnp.where(jnp.arange(DOMAIN_ATOMS, dtype=jnp.int32)[None, :] == picked_rows, NEIGHBOUR_SLOTS, count_values)
    return count_values.reshape(TOTAL_ATOMS).astype(jnp.int32)


def with_ends(drawn, stream_key, low, top_value):
    longest = drawn.shape.index(max(drawn.shape))
    spots = []
    for shift in (0, 1):
        where = [jax.random.randint(jax.random.fold_in(stream_key, axis), (), 0, length) for axis, length in enumerate(drawn.shape)]
        where[longest] = (where[longest] + shift) % drawn.shape[longest]
        spots.append(tuple(where))
    return drawn.at[spots[0]].set(low).at[spots[1]].set(top_value)


def levels(key, extent, cuts, smallest, largest):
    gain, own = 1.0, jax.random.fold_in(key, 6)
    for position, blocks in cuts:
        draws = jnp.exp(jax.random.uniform(jax.random.fold_in(own, position), (blocks,), jnp.float32, smallest / len(cuts), largest / len(cuts)))
        gain = gain * jnp.repeat(draws, extent[position] // blocks).reshape([-1 if axis == position else 1 for axis in range(len(extent))])
    return gain


def scatter_about(stream_key, extent, scale, most, kind=jnp.bfloat16):
    result = scale * jax.random.normal(stream_key, extent, jnp.float32)
    return jnp.clip(result, min=-most, max=most).astype(kind)


def setup_inputs(seed: int = 0) -> dict:
    arg_keys = jax.random.split(jax.random.key(seed), 15)
    return {
        "features": draw_features(jax.random.fold_in(arg_keys[14], 71), 0),
        "positions": draw_positions(jax.random.fold_in(arg_keys[14], 71), 0),
        "wave_vectors": draw_wave_vectors(jax.random.fold_in(arg_keys[14], 71), 0),
        "filter_width": jnp.clip(jnp.exp(jax.random.uniform(arg_keys[3], (C,), jnp.float32, math.log(0.002), math.log(0.02))), 0.002, 0.02),
        "w_charge": scatter_about(arg_keys[4], (FEATURE_WIDTH, C), FEATURE_WIDTH ** -0.5, 0.5),
        "w_filter_in": scatter_about(arg_keys[5], (NRBF, FEATURE_WIDTH), NRBF ** -0.5, 1.25),
        "filter_output_weight": scatter_about(arg_keys[6], (FEATURE_WIDTH, FEATURE_WIDTH), FEATURE_WIDTH ** -0.5, 0.5),
        "update_weight": scatter_about(arg_keys[7], (FEATURE_WIDTH, FEATURE_WIDTH), (FEATURE_WIDTH * NEIGHBOUR_SLOTS // 4) ** -0.5, 0.125),
        "w_long": scatter_about(arg_keys[8], (C, FEATURE_WIDTH), C ** -0.5, 1.5, jnp.float32),
        "send_along_x": draw_send_along_x(jax.random.fold_in(arg_keys[14], 71), 0),
        "send_along_y": draw_send_along_y(jax.random.fold_in(arg_keys[14], 71), 0),
        "neighbours": with_ends(jax.random.randint(arg_keys[11], (NEIGHBOUR_SLOTS, TOTAL_ATOMS), 0, DOMAIN_ATOMS + 4 * GHOST_ROWS), jax.random.fold_in(arg_keys[11], 1), 0, (DOMAIN_ATOMS + 4 * GHOST_ROWS) - 1).astype(jnp.int32),
        "neighbour_count": draw_neighbour_count(jax.random.fold_in(arg_keys[14], 71), 0),
        "distances": jnp.clip(0.8 + 4 * jax.random.uniform(arg_keys[13], (NEIGHBOUR_SLOTS, TOTAL_ATOMS), jnp.float32) ** levels(arg_keys[13], (NEIGHBOUR_SLOTS, TOTAL_ATOMS), ((1, 32),), -0.2, 0.2), 0.8, 4.8),
    }


two_pi = 2.0 * math.pi
force_unit = 0.001

def shifted_softplus(value):
    return jax.nn.softplus(value) - math.log(2.0)

def phase_table(k_piece, coords):
    kf = k_piece.astype(jnp.float32)
    angle = two_pi * (kf[0][:, None] * coords[0][None, :] + kf[1][:, None] * coords[1][None, :] + kf[2][:, None] * coords[2][None, :])
    return jnp.stack([jnp.cos(angle), jnp.sin(angle)]).astype(jnp.bfloat16)

def build_coefficients(structure, k_piece, filter_width):
    kf = k_piece.astype(jnp.float32)
    squared = two_pi * two_pi * (kf[0] * kf[0] + kf[1] * kf[1] + 0.25 * kf[2] * kf[2])
    weight = jnp.exp(-0.5 * (filter_width * filter_width)[:, None] * squared[None, :]) * (two_pi * two_pi / squared)[None, :]
    filtered = structure * weight[:, None, :]
    pieces = [filtered]
    for axis_index in range(3):
        factor = two_pi * kf[axis_index]
        pieces.append(jnp.stack([factor * filtered[:, 1], -factor * filtered[:, 0]], axis=1))
    return jnp.concatenate(pieces, axis=0).astype(jnp.bfloat16)

def ghost_tables(features, send_along_x, send_along_y):
    grid = features.reshape(N_GX, N_GY, DOMAIN_ATOMS, FEATURE_WIDTH)
    pick = jax.vmap(jax.vmap(lambda rows, chosen: jnp.take(rows, chosen, axis=0)))
    lists_x = send_along_x.reshape(2, N_GX, N_GY, GHOST_ROWS)
    from_minus = jnp.roll(pick(grid, lists_x[0]), 1, axis=0)
    from_plus = jnp.roll(pick(grid, lists_x[1]), -1, axis=0)
    first_table = jnp.concatenate([grid, from_minus, from_plus], axis=2)
    lists_y = send_along_y.reshape(2, N_GX, N_GY, GHOST_ROWS)
    from_minus = jnp.roll(pick(first_table, lists_y[0]), 1, axis=1)
    from_plus = jnp.roll(pick(first_table, lists_y[1]), -1, axis=1)
    ghost_table = jnp.concatenate([first_table, from_minus, from_plus], axis=2)
    return ghost_table.reshape(N_GX * N_GY, DOMAIN_ATOMS + 4 * GHOST_ROWS, FEATURE_WIDTH)

def local_messages(ghost_table, neighbour_ids, live_count, distance, w_filter_in, filter_output_weight):
    centers = 5.0 * jnp.arange(NRBF, dtype=jnp.float32) / (NRBF - 1)
    sharpness = 0.02 * (NRBF - 1) * (NRBF - 1)
    offsets = distance[..., None] - centers
    radial_basis = jnp.exp(-sharpness * offsets * offsets).astype(jnp.bfloat16)
    hidden_features = shifted_softplus(jnp.dot(radial_basis.reshape(-1, NRBF), w_filter_in, preferred_element_type=jnp.float32)).astype(jnp.bfloat16)
    filter_values = jnp.dot(hidden_features, filter_output_weight, preferred_element_type=jnp.float32).reshape(NEIGHBOUR_SLOTS, DOMAIN_ATOMS, FEATURE_WIDTH)
    neighbour_rows = jnp.take(ghost_table, neighbour_ids, axis=0).astype(jnp.float32)
    slots = lax.broadcasted_iota(jnp.int32, neighbour_ids.shape, 0)
    envelope = jnp.where(slots < live_count[None, :], 0.5 * (jnp.cos(math.pi * distance / 5.0) + 1.0), 0.0)
    return lax.optimization_barrier(jnp.sum(envelope[..., None] * neighbour_rows * filter_values, axis=0))

def reference(features, positions, wave_vectors, filter_width, w_charge, w_filter_in, filter_output_weight, update_weight, w_long, send_along_x, send_along_y, neighbours, neighbour_count, distances):
    domain_list = N_GX * N_GY
    charges = jnp.dot(features, w_charge, preferred_element_type=jnp.float32).astype(jnp.bfloat16).T
    mean_charge = lax.optimization_barrier(jnp.sum(charges.astype(jnp.float32), axis=1)) / TOTAL_ATOMS
    charge_blocks = charges.reshape(C, domain_list, DOMAIN_ATOMS).transpose(1, 0, 2)
    coord_blocks = positions.reshape(3, domain_list, DOMAIN_ATOMS).transpose(1, 0, 2)
    unit_row = jnp.ones((1, DOMAIN_ATOMS), jnp.bfloat16)

    def add_block(running, pieces):
        block_charges, block_coords = pieces
        wave_table = phase_table(wave_vectors, block_coords).reshape(2 * K, DOMAIN_ATOMS)
        extended = jnp.concatenate([block_charges, unit_row], axis=0)
        return (running + jnp.dot(extended, wave_table.T, preferred_element_type=jnp.float32), None)
    raw, unused = lax.scan(add_block, jnp.zeros((C + 1, 2 * K), jnp.float32), (charge_blocks, coord_blocks))
    raw = raw.reshape(C + 1, 2, K)
    structure = raw[:C] - mean_charge[:, None, None] * raw[C][None]
    coefficients = build_coefficients(structure, wave_vectors, filter_width).reshape(4 * C, 2 * K)
    inv_root = 1.0 / math.sqrt(TOTAL_ATOMS)

    def project(block_coords):
        wave_table = phase_table(wave_vectors, block_coords).reshape(2 * K, DOMAIN_ATOMS)
        return jnp.dot(coefficients, wave_table, preferred_element_type=jnp.float32) * inv_root
    fields = lax.map(project, coord_blocks)
    tables = ghost_tables(features, send_along_x, send_along_y)
    identity_blocks = neighbours.reshape(NEIGHBOUR_SLOTS, domain_list, DOMAIN_ATOMS).transpose(1, 0, 2)
    distance_blocks = distances.reshape(NEIGHBOUR_SLOTS, domain_list, DOMAIN_ATOMS).transpose(1, 0, 2)
    count_blocks = neighbour_count.reshape(domain_list, DOMAIN_ATOMS)

    def domain_messages(pieces):
        table, ids, count_values, lengths = pieces
        return local_messages(table, ids, count_values, lengths, w_filter_in, filter_output_weight)
    messages = lax.map(domain_messages, (tables, identity_blocks, count_blocks, distance_blocks))
    messages = messages.reshape(TOTAL_ATOMS, FEATURE_WIDTH).astype(jnp.bfloat16)
    potentials = fields[:, :C].transpose(0, 2, 1).reshape(TOTAL_ATOMS, C)
    updated = features.astype(jnp.float32) + jnp.dot(messages, update_weight, preferred_element_type=jnp.float32)
    updated = updated + jnp.dot(potentials, w_long, precision=lax.Precision.HIGHEST)
    centred = charge_blocks.astype(jnp.float32) - mean_charge[None, :, None]
    field_parts = fields[:, C:].reshape(domain_list, 3, C, DOMAIN_ATOMS)
    forces = -force_unit * lax.optimization_barrier(jnp.sum(centred[:, None] * field_parts, axis=2))
    forces = forces.transpose(1, 0, 2).reshape(3, TOTAL_ATOMS)
    return (updated.astype(jnp.bfloat16), forces)
```

```python
import math

import jax
import jax.numpy as jnp
from jax import lax
from jax.experimental import pallas as pl
from jax.experimental.pallas import tpu as pltpu
from jax.sharding import PartitionSpec as P

two_pi = 2.0 * math.pi
force_unit = 0.001
f32 = jnp.float32
bf16 = jnp.bfloat16

sin_terms = (4.442867902992535, -7.307443419719773, 3.594788063370906, -0.7843739903522723)
cos_terms = (1.414204080647301, -6.977642060724434, 5.715238411759286, -1.7283486673792663)

cos_scale = sin_terms[3] * sin_terms[3]
sin_scale = sin_terms[3] * cos_terms[3]

rounder = 1.5 * 2.0**23

payload_rows = 24
part_rows = ((0, 3), (3, 3), (6, 2))
result_rows = 24


def dot(a, b, contract, precision=None):
    return lax.dot_general(
        a, b, (contract, ((), ())), preferred_element_type=f32, precision=precision
    )


def passed_along(block, axis, distance):
    devices = range(lax.axis_size(axis))
    route = [((i - distance) % len(devices), i) for i in devices]
    return lax.ppermute(block, axis, route)


def place():
    return lax.axis_index("gx") * lax.axis_size("gy") + lax.axis_index("gy")


def over_devices(blocks):
    return lax.all_to_all(blocks, ("gx", "gy"), 0, 0, tiled=True)


def waves_of(turns):
    part = turns - ((turns + rounder) - rounder)
    square = part * part
    sine = part * polynomial(sin_terms, square)
    cosine = polynomial(cos_terms, square)
    return 1.0 / cos_scale - sine * sine, sine * cosine


def polynomial(terms, square):
    value = square + terms[2] / terms[3]
    for term in terms[1::-1]:
        value = value * square + term / terms[3]
    return value


def picked(list_row, tables):
    total, first = None, 0
    for table in tables:
        rows = table.shape[0]
        ids = lax.broadcasted_iota(jnp.int32, (rows, list_row.shape[1]), 0) + first
        chosen = jnp.where(ids == list_row, 1.0, 0.0).astype(bf16)
        part = dot(chosen, table, ((0,), (0,)))
        total = part if total is None else total + part
        first += rows
    return total


def fetched(given, held, semaphores):
    moves = [
        pltpu.make_async_copy(source, target, semaphores.at[i]) for i, (source, target) in enumerate(zip(given, held))
    ]
    for move in moves:
        move.start()
    for move in moves:
        move.wait()


def hold_kernel(*refs):
    count = (len(refs) - 1) // 2
    fetched(refs[:count], refs[count:-1], refs[-1])


def send_kernel(*refs):
    given, (copies_ref, minus_ref, plus_ref) = refs[:4], refs[4:7]
    held, rows_ref, semaphores = refs[7:11], refs[11], refs[12]
    fetched(given, held, semaphores)
    features_ref, positions_ref, w_charge_ref, lists_ref = held
    features = features_ref[...]
    channels = w_charge_ref.shape[0]
    charges = dot(w_charge_ref[...], features, ((1,), (1,))).astype(bf16).astype(f32)
    rows_ref[...] = jnp.zeros_like(rows_ref)
    rows_ref[0:channels, :] = charges
    left = positions_ref[...]
    for first, rows in part_rows:
        rounded = left.astype(bf16).astype(f32)
        rows_ref[channels + first : channels + first + rows, :] = rounded[:rows]
        left = left - rounded
    block = rows_ref[...].astype(bf16)

    def place(index, unused):
        copies_ref[index] = block
        return unused

    lax.fori_loop(0, copies_ref.shape[0], place, 0, unroll=8)
    minus_ref[...] = picked(lists_ref[0:1, :], [features]).astype(bf16)
    plus_ref[...] = picked(lists_ref[1:2, :], [features]).astype(bf16)


def second_send_kernel(features_ref, from_minus_ref, from_plus_ref, lists_ref, minus_ref, plus_ref):
    tables = [features_ref[...], from_minus_ref[...], from_plus_ref[...]]
    for direction, result_ref in enumerate((minus_ref, plus_ref)):
        result_ref[...] = picked(lists_ref[direction : direction + 1, :], tables).astype(bf16)


def factors_kernel(channels, vectors_ref, width_ref, integers_ref, factors_ref, held_ref, held_width_ref, semaphores):
    count = integers_ref.shape[0]
    window = held_ref.shape[1]
    offset = place() * count
    first = pl.multiple_of(offset // window * window, window)
    fetched((vectors_ref.at[:, pl.ds(first, window)], width_ref), (held_ref, held_width_ref), semaphores)
    vectors = held_ref[...].astype(f32)
    if window > count:
        vectors = pltpu.roll(vectors, lax.rem(window - (offset - first), window), 1)[:, :count]
    kx, ky, kz = vectors[0:1], vectors[1:2], vectors[2:3]
    squared = two_pi * two_pi * (kx * kx + ky * ky + 0.25 * kz * kz)
    diagonal = lax.broadcasted_iota(jnp.int32, (channels, channels), 0) == lax.broadcasted_iota(
        jnp.int32, (channels, channels), 1
    )
    width = jnp.sum(jnp.where(diagonal, held_width_ref[...], 0.0), axis=1, keepdims=True)
    weight = jnp.exp(-0.5 * (width * width) * squared) * (two_pi * two_pi / squared)
    factors_ref[...] = jnp.concatenate([weight] + [two_pi * along * weight for along in (kx, ky, kz)], axis=0)
    component = lax.broadcasted_iota(jnp.int32, (payload_rows, count), 0) - channels
    inside = (component >= 0) & (component < 8)
    component = lax.rem(jnp.maximum(component, 0), 3)
    integers = jnp.where(component == 0, kx, jnp.where(component == 1, ky, kz))
    integers_ref[...] = jnp.where(inside, integers, 0.0).T.astype(bf16)


per_tile = 4


def tile_of(blocks_ref, index):
    return jnp.concatenate([blocks_ref[per_tile * index + i] for i in range(per_tile)], axis=1)


def add_waves(channels, blocks_ref, integers_ref, waves_ref, joined_ref, weights_ref, turns_ref):
    devices, rows, own = blocks_ref.shape
    count = integers_ref.shape[0]
    chunk = min(count, 128)
    weights_ref[channels : 2 * channels, :] = jnp.ones((channels, devices * own), bf16)
    weights_ref[2 * channels :, :] = jnp.zeros((128 - 2 * channels, devices * own), bf16)

    def join(index, unused):
        lanes = pl.ds(pl.multiple_of(index * own, own), own)
        block = blocks_ref[index]
        joined_ref[:, lanes] = block
        weights_ref[0:channels, lanes] = block[:channels]
        return unused

    lax.fori_loop(0, devices, join, 0, unroll=8)
    turns_ref[...] = dot(integers_ref[...], joined_ref[...], ((1,), (0,)))

    def step(index, unused):
        for part in range(2):
            lanes = pl.ds(pl.multiple_of((2 * index + part) * own, own), own)
            for first in range(0, count, chunk):
                cosine, sine = waves_of(turns_ref[first : first + chunk, lanes])
                waves_ref[first : first + chunk, lanes] = cosine.astype(bf16)
                waves_ref[count + first : count + first + chunk, lanes] = sine.astype(bf16)
        return unused

    lax.fori_loop(0, devices // 2, step, 0)
    return [
        dot(waves_ref[wave * count : (wave + 1) * count, :], weights_ref[...], ((1,), (1,))) for wave in range(2)
    ]


def put_fields(channels, atoms, blocks_ref, waves_ref, coefficients_ref, mean, result_ref):
    devices, _, own = blocks_ref.shape
    count = coefficients_ref.shape[2]
    wide = per_tile * own
    scale = 1.0 / math.sqrt(atoms)

    def waves_at(index, wave):
        lanes = pl.ds(pl.multiple_of(index * wide, wide), wide)
        return waves_ref[wave * count : (wave + 1) * count, lanes]

    def step(turn, unused):
        indices = (2 * turn, 2 * turn + 1)
        fields_of = [
            sum(dot(coefficients_ref[wave], waves_at(index, wave), ((1,), (0,))) for wave in range(2))
            for index in indices
        ]
        for index, fields in zip(indices, fields_of):
            fields = fields * scale
            centred = tile_of(blocks_ref, index)[:channels].astype(f32) - mean
            rows = [fields[:channels]]
            for axis in range(3):
                along = fields[(axis + 1) * channels : (axis + 2) * channels]
                rows.append(-force_unit * jnp.sum(centred * along, axis=0, keepdims=True))
            rows.append(jnp.zeros((result_rows - channels - 3, wide), f32))
            result = jnp.concatenate(rows, axis=0)
            for i in range(per_tile):
                result_ref[per_tile * index + i] = result[:, i * own : (i + 1) * own].astype(result_ref.dtype)
        return unused

    lax.fori_loop(0, devices // (2 * per_tile), step, 0)


def waves_kernel(channels, gathered_ref, integers_ref, factors_ref, result_ref, waves_ref, coefficients_ref, *scratch):
    devices, _, own = gathered_ref.shape
    atoms = devices * own
    sums = [total.T for total in add_waves(channels, gathered_ref, integers_ref, waves_ref, *scratch)]

    def add_up(index, total):
        return total + gathered_ref[index][:channels].astype(f32)

    total = lax.fori_loop(0, devices, add_up, jnp.zeros((channels, own), f32), unroll=8)
    mean = jnp.sum(total, axis=1, keepdims=True) * (1.0 / atoms)
    cosine, sine = [total[0:channels, :] - mean * total[channels : channels + 1, :] for total in sums]
    cosine, sine = cosine * cos_scale, sine * sin_scale
    factors = factors_ref[...]
    coefficients_ref[0] = (cos_scale * factors * jnp.concatenate([cosine] + [sine] * 3, axis=0)).astype(bf16)
    coefficients_ref[1] = (sin_scale * factors * jnp.concatenate([sine] + [-cosine] * 3, axis=0)).astype(bf16)
    put_fields(channels, atoms, gathered_ref, waves_ref, coefficients_ref, mean, result_ref)


filter_group = 32


def filters_kernel(count_ref, distances_ref, w_in_ref, w_out_ref, filters_ref, radial_ref, envelope_ref):
    slots, own = distances_ref.shape
    radial = w_in_ref.shape[0]
    radial_ref[...] = jnp.zeros_like(radial_ref)
    radial_ref[0:radial, :] = w_in_ref[...].astype(f32)
    w_in = radial_ref[...].T.astype(bf16)
    w_out = w_out_ref[...].astype(f32).T.astype(bf16)
    padded = radial_ref.shape[0]
    centers = 5.0 * lax.broadcasted_iota(jnp.int32, (padded, own), 0).astype(f32) / (radial - 1)
    sharpness = 0.02 * (radial - 1) * (radial - 1)
    live = lax.broadcasted_iota(jnp.int32, (slots, own), 0) < count_ref[...]
    envelope_ref[...] = jnp.where(live, 0.5 * (cos_scale * waves_of(0.1 * distances_ref[...])[0] + 1.0), 0.0)
    pairs = range(0, filter_group, 2)

    def step(turn, unused):
        start = pl.multiple_of(turn * filter_group, filter_group)
        lengths = distances_ref[pl.ds(start, filter_group), :]
        envelope = envelope_ref[pl.ds(start, filter_group), :]
        values, filters = [], []
        for pair in pairs:
            basis = []
            for slot in (pair, pair + 1):
                offsets = lengths[slot : slot + 1] - centers
                basis.append(jnp.exp(-sharpness * offsets * offsets).astype(bf16))
            values.append(dot(w_in, jnp.concatenate(basis, axis=1), ((1,), (0,))))
        for value in values:
            hidden = (jnp.log(1.0 + jnp.exp(value)) - math.log(2.0)).astype(bf16)
            filters.append(dot(w_out, hidden, ((1,), (0,))))
        for slot in range(filter_group):
            lanes = slice(slot % 2 * own, (slot % 2 + 1) * own)
            filters_ref[start + slot] = envelope[slot : slot + 1] * filters[slot // 2][:, lanes]
        return unused

    lax.fori_loop(0, slots // filter_group, step, 0)


def messages_kernel(
    features_ref, x_minus_ref, x_plus_ref, y_minus_ref, y_plus_ref, neighbours_ref, filters_ref, w_update_ref,
    result_ref, table_ref,
):
    slots, own = neighbours_ref.shape
    width = features_ref.shape[1]
    first = 0
    for part in (features_ref, x_minus_ref, x_plus_ref, y_minus_ref, y_plus_ref):
        table_ref[first : first + part.shape[0], :] = part[...].astype(f32)
        first += part.shape[0]
    table = table_ref[...].T.astype(bf16)
    row_ids = lax.broadcasted_iota(jnp.int32, (first, own), 0).astype(f32).astype(bf16)
    ones, zeros = jnp.ones((first, own), bf16), jnp.zeros((first, own), bf16)

    ids = neighbours_ref[...].astype(f32)
    rows = []
    for pair in range(0, slots, 2):
        chosen = []
        for slot in (pair, pair + 1):
            wanted = jnp.broadcast_to(ids[slot : slot + 1], (16, own)).astype(bf16)
            wanted = jnp.concatenate([wanted] * (first // 16), axis=0)
            chosen.append(jnp.where(row_ids == wanted, ones, zeros))
        rows.append(dot(table, jnp.concatenate(chosen, axis=1), ((1,), (0,))))
    total = jnp.zeros((width, own), f32)
    for slot in range(slots):
        lanes = slice(slot % 2 * own, (slot % 2 + 1) * own)
        total = total + rows[slot // 2][:, lanes] * filters_ref[slot]
    update = dot(total.T.astype(bf16), w_update_ref[...], ((1,), (0,)))
    result_ref[...] = features_ref[...].astype(f32) + update


def final_kernel(channels, base_ref, summed_ref, w_long_ref, updated_ref, forces_ref):
    summed = jnp.sum(summed_ref[...].astype(f32), axis=0)
    potentials = summed[:channels].T
    long_range = dot(potentials, w_long_ref[...], ((1,), (0,)), lax.Precision.HIGHEST)
    updated_ref[...] = (base_ref[...] + long_range).astype(bf16)
    forces_ref[...] = summed[channels : channels + 3]


def per_device(
    features, positions, wave_vectors, filter_width, w_charge, w_filter_in, filter_output_weight,
    update_weight, w_long, send_along_x, send_along_y, neighbours, neighbour_count, distances,
):
    own, width = features.shape
    channels = w_charge.shape[1]
    devices = lax.axis_size("gx") * lax.axis_size("gy")
    count = wave_vectors.shape[1] // devices
    ghosts = send_along_x.shape[1]
    struct = jax.ShapeDtypeStruct
    small = pltpu.CompilerParams(vmem_limit_bytes=24 * 1024 * 1024)

    copies, x_minus, x_plus = pl.pallas_call(
        send_kernel,
        out_shape=(
            struct((devices, payload_rows, own), bf16), struct((ghosts, width), bf16), struct((ghosts, width), bf16),
        ),
        in_specs=[pl.BlockSpec(memory_space=pltpu.HBM)] * 4,
        scratch_shapes=[
            pltpu.VMEM((own, width), bf16),
            pltpu.VMEM((3, own), f32),
            pltpu.VMEM((channels, width), bf16),
            pltpu.VMEM(send_along_x.shape, jnp.int32),
            pltpu.VMEM((payload_rows, own), f32),
            pltpu.SemaphoreType.DMA((4,)),
        ],
        compiler_params=small,
        name="send",
    )(*[
        pltpu.with_memory_space_constraint(array, pltpu.HBM)
        for array in (features, positions, w_charge.T, send_along_x)
    ])

    x_minus = passed_along(x_minus, "gx", 1)
    x_plus = passed_along(x_plus, "gx", -1)
    integers, factors = pl.pallas_call(
        lambda *refs: factors_kernel(channels, *refs),
        out_shape=(struct((count, payload_rows), bf16), struct((4 * channels, count), f32)),
        in_specs=[pl.BlockSpec(memory_space=pltpu.HBM)] * 2,
        scratch_shapes=[
            pltpu.VMEM((wave_vectors.shape[0], max(count, 128)), jnp.int32),
            pltpu.VMEM((1, channels), f32),
            pltpu.SemaphoreType.DMA((2,)),
        ],
        compiler_params=small,
        name="factors",
    )(*[pltpu.with_memory_space_constraint(array, pltpu.HBM) for array in (wave_vectors, filter_width[None, :])])

    later = (
        features, send_along_y, neighbours, neighbour_count[None, :], distances,
        w_filter_in, filter_output_weight, update_weight, w_long,
    )
    later = pl.pallas_call(
        hold_kernel,
        out_shape=tuple(struct(array.shape, array.dtype) for array in later),
        in_specs=[pl.BlockSpec(memory_space=pltpu.HBM)] * len(later),
        scratch_shapes=[pltpu.SemaphoreType.DMA((len(later),))],
        compiler_params=small,
        name="hold",
    )(*[pltpu.with_memory_space_constraint(array, pltpu.HBM) for array in later])
    gathered, x_minus, x_plus, integers, factors, later = lax.optimization_barrier(
        (over_devices(copies), x_minus, x_plus, integers, factors, later)
    )
    (
        features, send_along_y, neighbours, neighbour_count, distances,
        w_filter_in, filter_output_weight, update_weight, w_long,
    ) = later
    held_bytes = devices * own * (8 * count + 2 * (128 + 2 * payload_rows + result_rows))
    partial = pl.pallas_call(
        lambda *refs: waves_kernel(channels, *refs),
        out_shape=struct((devices, result_rows, own), bf16),
        scratch_shapes=[
            pltpu.VMEM((2 * count, devices * own), bf16),
            pltpu.VMEM((2, 4 * channels, count), bf16),
            pltpu.VMEM((payload_rows, devices * own), bf16),
            pltpu.VMEM((128, devices * own), bf16),
            pltpu.VMEM((count, devices * own), f32),
        ],
        compiler_params=pltpu.CompilerParams(vmem_limit_bytes=held_bytes + 8 * 1024 * 1024),
        cost_estimate=pl.CostEstimate(flops=40 * count * devices * own, bytes_accessed=1 << 20, transcendentals=0),
        name="waves",
    )(gathered, integers, factors)
    partial, x_minus, x_plus = lax.optimization_barrier((partial, x_minus, x_plus))
    received = over_devices(partial)

    y_minus, y_plus = pl.pallas_call(
        second_send_kernel,
        out_shape=(struct((ghosts, width), bf16), struct((ghosts, width), bf16)),
        compiler_params=small,
        name="second_send",
    )(features, x_minus, x_plus, send_along_y)
    y_minus = passed_along(y_minus, "gy", 1)
    y_plus = passed_along(y_plus, "gy", -1)
    slots = neighbours.shape[0]
    distances, w_filter_in, x_minus = lax.optimization_barrier((distances, w_filter_in, x_minus))
    filters = pl.pallas_call(
        filters_kernel,
        out_shape=struct((slots, width, own), f32),
        scratch_shapes=[pltpu.VMEM((32, width), f32), pltpu.VMEM(distances.shape, f32)],
        compiler_params=small,
        cost_estimate=pl.CostEstimate(
            flops=2 * slots * own * width * width, bytes_accessed=1 << 20, transcendentals=2 * slots * own * width
        ),
        name="filters",
    )(neighbour_count, distances, w_filter_in, filter_output_weight)
    filters, y_minus, y_plus = lax.optimization_barrier((filters, y_minus, y_plus))
    base = pl.pallas_call(
        messages_kernel,
        out_shape=struct((own, width), f32),
        scratch_shapes=[pltpu.VMEM((own + 4 * ghosts, width), f32)],
        compiler_params=small,
        cost_estimate=pl.CostEstimate(
            flops=2 * slots * own * width * 256, bytes_accessed=1 << 20, transcendentals=0
        ),
        name="messages",
    )(features, x_minus, x_plus, y_minus, y_plus, neighbours, filters, update_weight)

    updated, forces = pl.pallas_call(
        lambda *refs: final_kernel(channels, *refs),
        out_shape=(struct((own, width), bf16), struct((3, own), f32)),
        compiler_params=small,
        name="final",
    )(base, received, w_long)
    return updated, forces


def solution(mesh):
    placed = (
        P(("gx", "gy"), None),
        P(None, ("gx", "gy")),
        P(),
        P(),
        P(),
        P(),
        P(),
        P(),
        P(),
        P(None, ("gx", "gy")),
        P(None, ("gx", "gy")),
        P(None, ("gx", "gy")),
        P(("gx", "gy")),
        P(None, ("gx", "gy")),
    )
    return jax.shard_map(
        per_device,
        mesh=mesh,
        in_specs=placed,
        out_specs=(P(("gx", "gy"), None), P(None, ("gx", "gy"))),
        check_vma=False,
    )
```

```python
import math

import jax
import jax.numpy as jnp
from jax import lax
from jax.experimental import pallas as pl
from jax.experimental.pallas import tpu as pltpu
from jax.sharding import PartitionSpec as P

two_pi = 2.0 * math.pi
force_unit = 0.001
f32 = jnp.float32
bf16 = jnp.bfloat16

sin_terms = (4.442867902992535, -7.307443419719773, 3.594788063370906, -0.7843739903522723)
cos_terms = (1.414204080647301, -6.977642060724434, 5.715238411759286, -1.7283486673792663)

cos_scale = sin_terms[3] * sin_terms[3]
sin_scale = sin_terms[3] * cos_terms[3]

rounder = 1.5 * 2.0**23

payload_rows = 24
part_rows = ((0, 3), (3, 3), (6, 2))
result_rows = 24


def dot(a, b, contract, precision=None):
    return lax.dot_general(
        a, b, (contract, ((), ())), preferred_element_type=f32, precision=precision
    )


def passed_along(block, axis, distance):
    devices = range(lax.axis_size(axis))
    route = [((i - distance) % len(devices), i) for i in devices]
    return lax.ppermute(block, axis, route)


def place():
    return lax.axis_index("gx") * lax.axis_size("gy") + lax.axis_index("gy")


def over_devices(blocks):
    return lax.all_to_all(blocks, ("gx", "gy"), 0, 0, tiled=True)


def waves_of(turns):
    part = turns - ((turns + rounder) - rounder)
    square = part * part
    sine = part * polynomial(sin_terms, square)
    cosine = polynomial(cos_terms, square)
    return 1.0 / cos_scale - sine * sine, sine * cosine


def polynomial(terms, square):
    value = square + terms[2] / terms[3]
    for term in terms[1::-1]:
        value = value * square + term / terms[3]
    return value


def picked(list_row, tables):
    total, first = None, 0
    for table in tables:
        rows = table.shape[0]
        ids = lax.broadcasted_iota(jnp.int32, (rows, list_row.shape[1]), 0) + first
        chosen = jnp.where(ids == list_row, 1.0, 0.0).astype(bf16)
        part = dot(chosen, table, ((0,), (0,)))
        total = part if total is None else total + part
        first += rows
    return total


def fetched(given, held, semaphores):
    moves = [
        pltpu.make_async_copy(source, target, semaphores.at[i]) for i, (source, target) in enumerate(zip(given, held))
    ]
    for move in moves:
        move.start()
    for move in moves:
        move.wait()


def hold_kernel(*refs):
    count = (len(refs) - 1) // 2
    fetched(refs[:count], refs[count:-1], refs[-1])


def send_kernel(*refs):
    given, (copies_ref, minus_ref, plus_ref) = refs[:4], refs[4:7]
    held, rows_ref, semaphores = refs[7:11], refs[11], refs[12]
    fetched(given, held, semaphores)
    features_ref, positions_ref, w_charge_ref, lists_ref = held
    features = features_ref[...]
    channels = w_charge_ref.shape[0]
    charges = dot(w_charge_ref[...], features, ((1,), (1,))).astype(bf16).astype(f32)
    rows_ref[...] = jnp.zeros_like(rows_ref)
    rows_ref[0:channels, :] = charges
    left = positions_ref[...]
    for first, rows in part_rows:
        rounded = left.astype(bf16).astype(f32)
        rows_ref[channels + first : channels + first + rows, :] = rounded[:rows]
        left = left - rounded
    block = rows_ref[...].astype(bf16)

    def place(index, unused):
        copies_ref[index] = block
        return unused

    lax.fori_loop(0, copies_ref.shape[0], place, 0, unroll=8)
    minus_ref[...] = picked(lists_ref[0:1, :], [features]).astype(bf16)
    plus_ref[...] = picked(lists_ref[1:2, :], [features]).astype(bf16)


def second_send_kernel(features_ref, from_minus_ref, from_plus_ref, lists_ref, minus_ref, plus_ref):
    tables = [features_ref[...], from_minus_ref[...], from_plus_ref[...]]
    for direction, result_ref in enumerate((minus_ref, plus_ref)):
        result_ref[...] = picked(lists_ref[direction : direction + 1, :], tables).astype(bf16)


def factors_kernel(channels, vectors_ref, width_ref, integers_ref, factors_ref, held_ref, held_width_ref, semaphores):
    count = integers_ref.shape[0]
    window = held_ref.shape[1]
    offset = place() * count
    first = pl.multiple_of(offset // window * window, window)
    fetched((vectors_ref.at[:, pl.ds(first, window)], width_ref), (held_ref, held_width_ref), semaphores)
    vectors = held_ref[...].astype(f32)
    if window > count:
        vectors = pltpu.roll(vectors, lax.rem(window - (offset - first), window), 1)[:, :count]
    kx, ky, kz = vectors[0:1], vectors[1:2], vectors[2:3]
    squared = two_pi * two_pi * (kx * kx + ky * ky + 0.25 * kz * kz)
    diagonal = lax.broadcasted_iota(jnp.int32, (channels, channels), 0) == lax.broadcasted_iota(
        jnp.int32, (channels, channels), 1
    )
    width = jnp.sum(jnp.where(diagonal, held_width_ref[...], 0.0), axis=1, keepdims=True)
    weight = jnp.exp(-0.5 * (width * width) * squared) * (two_pi * two_pi / squared)
    factors_ref[...] = jnp.concatenate([weight] + [two_pi * along * weight for along in (kx, ky, kz)], axis=0)
    component = lax.broadcasted_iota(jnp.int32, (payload_rows, count), 0) - channels
    inside = (component >= 0) & (component < 8)
    component = lax.rem(jnp.maximum(component, 0), 3)
    integers = jnp.where(component == 0, kx, jnp.where(component == 1, ky, kz))
    integers_ref[...] = jnp.where(inside, integers, 0.0).T.astype(bf16)


per_tile = 4


def tile_of(blocks_ref, index):
    return jnp.concatenate([blocks_ref[per_tile * index + i] for i in range(per_tile)], axis=1)


def add_waves(channels, blocks_ref, integers_ref, waves_ref, joined_ref, weights_ref, turns_ref):
    devices, rows, own = blocks_ref.shape
    count = integers_ref.shape[0]
    chunk = min(count, 128)
    weights_ref[channels : 2 * channels, :] = jnp.ones((channels, devices * own), bf16)
    weights_ref[2 * channels :, :] = jnp.zeros((128 - 2 * channels, devices * own), bf16)

    def join(index, unused):
        lanes = pl.ds(pl.multiple_of(index * own, own), own)
        block = blocks_ref[index]
        joined_ref[:, lanes] = block
        weights_ref[0:channels, lanes] = block[:channels]
        return unused

    lax.fori_loop(0, devices, join, 0, unroll=8)
    turns_ref[...] = dot(integers_ref[...], joined_ref[...], ((1,), (0,)))

    def step(index, unused):
        for part in range(8):
            lanes = pl.ds(pl.multiple_of((8 * index + part) * own, own), own)
            for first in range(0, count, chunk):
                cosine, sine = waves_of(turns_ref[first : first + chunk, lanes])
                waves_ref[first : first + chunk, lanes] = cosine.astype(bf16)
                waves_ref[count + first : count + first + chunk, lanes] = sine.astype(bf16)
        return unused

    lax.fori_loop(0, devices // 8, step, 0)
    return [
        dot(waves_ref[wave * count : (wave + 1) * count, :], weights_ref[...], ((1,), (1,))) for wave in range(2)
    ]


def put_fields(channels, atoms, blocks_ref, waves_ref, coefficients_ref, mean, result_ref):
    devices, _, own = blocks_ref.shape
    count = coefficients_ref.shape[2]
    wide = per_tile * own
    scale = 1.0 / math.sqrt(atoms)

    def waves_at(index, wave):
        lanes = pl.ds(pl.multiple_of(index * wide, wide), wide)
        return waves_ref[wave * count : (wave + 1) * count, lanes]

    def step(turn, unused):
        indices = [4 * turn + i for i in range(4)]
        fields_of = [
            sum(dot(coefficients_ref[wave], waves_at(index, wave), ((1,), (0,))) for wave in range(2))
            for index in indices
        ]
        for index, fields in zip(indices, fields_of):
            fields = fields * scale
            centred = tile_of(blocks_ref, index)[:channels].astype(f32) - mean
            rows = [fields[:channels]]
            for axis in range(3):
                along = fields[(axis + 1) * channels : (axis + 2) * channels]
                rows.append(-force_unit * jnp.sum(centred * along, axis=0, keepdims=True))
            rows.append(jnp.zeros((result_rows - channels - 3, wide), f32))
            result = jnp.concatenate(rows, axis=0)
            for i in range(per_tile):
                result_ref[per_tile * index + i] = result[:, i * own : (i + 1) * own].astype(result_ref.dtype)
        return unused

    lax.fori_loop(0, devices // (4 * per_tile), step, 0)


def waves_kernel(channels, gathered_ref, integers_ref, factors_ref, result_ref, waves_ref, coefficients_ref, *scratch):
    devices, _, own = gathered_ref.shape
    atoms = devices * own
    sums = [total.T for total in add_waves(channels, gathered_ref, integers_ref, waves_ref, *scratch)]

    def add_up(index, total):
        return total + gathered_ref[index][:channels].astype(f32)

    total = lax.fori_loop(0, devices, add_up, jnp.zeros((channels, own), f32), unroll=8)
    mean = jnp.sum(total, axis=1, keepdims=True) * (1.0 / atoms)
    cosine, sine = [total[0:channels, :] - mean * total[channels : channels + 1, :] for total in sums]
    cosine, sine = cosine * cos_scale, sine * sin_scale
    factors = factors_ref[...]
    coefficients_ref[0] = (cos_scale * factors * jnp.concatenate([cosine] + [sine] * 3, axis=0)).astype(bf16)
    coefficients_ref[1] = (sin_scale * factors * jnp.concatenate([sine] + [-cosine] * 3, axis=0)).astype(bf16)
    put_fields(channels, atoms, gathered_ref, waves_ref, coefficients_ref, mean, result_ref)


filter_group = 32


def filters_kernel(count_ref, distances_ref, w_in_ref, w_out_ref, filters_ref, radial_ref, envelope_ref):
    slots, own = distances_ref.shape
    radial = w_in_ref.shape[0]
    radial_ref[...] = jnp.zeros_like(radial_ref)
    radial_ref[0:radial, :] = w_in_ref[...].astype(f32)
    w_in = radial_ref[...].T.astype(bf16)
    w_out = w_out_ref[...].astype(f32).T.astype(bf16)
    padded = radial_ref.shape[0]
    centers = 5.0 * lax.broadcasted_iota(jnp.int32, (padded, own), 0).astype(f32) / (radial - 1)
    sharpness = 0.02 * (radial - 1) * (radial - 1)
    live = lax.broadcasted_iota(jnp.int32, (slots, own), 0) < count_ref[...]
    envelope_ref[...] = jnp.where(live, 0.5 * (cos_scale * waves_of(0.1 * distances_ref[...])[0] + 1.0), 0.0)
    pairs = range(0, filter_group, 2)

    def step(turn, unused):
        start = pl.multiple_of(turn * filter_group, filter_group)
        lengths = distances_ref[pl.ds(start, filter_group), :]
        envelope = envelope_ref[pl.ds(start, filter_group), :]
        values, filters = [], []
        for pair in pairs:
            basis = []
            for slot in (pair, pair + 1):
                offsets = lengths[slot : slot + 1] - centers
                basis.append(jnp.exp(-sharpness * offsets * offsets).astype(bf16))
            values.append(dot(w_in, jnp.concatenate(basis, axis=1), ((1,), (0,))))
        for value in values:
            hidden = (jnp.log(1.0 + jnp.exp(value)) - math.log(2.0)).astype(bf16)
            filters.append(dot(w_out, hidden, ((1,), (0,))))
        for slot in range(filter_group):
            lanes = slice(slot % 2 * own, (slot % 2 + 1) * own)
            filters_ref[start + slot] = envelope[slot : slot + 1] * filters[slot // 2][:, lanes]
        return unused

    lax.fori_loop(0, slots // filter_group, step, 0)


def neighbour_sum(parts, first, neighbours_ref, filters_ref, table_ref, total):
    slots, own = neighbours_ref.shape
    count = table_ref.shape[0]
    filled = 0
    for part in parts:
        table_ref[filled : filled + part.shape[0], :] = part[...].astype(f32)
        filled += part.shape[0]
    table = table_ref[...].T.astype(bf16)
    row_ids = (lax.broadcasted_iota(jnp.int32, (count, own), 0) + first).astype(f32).astype(bf16)
    ones, zeros = jnp.ones((count, own), bf16), jnp.zeros((count, own), bf16)
    ids = neighbours_ref[...].astype(f32)
    rows = []
    for pair in range(0, slots, 2):
        chosen = []
        for slot in (pair, pair + 1):
            wanted = jnp.broadcast_to(ids[slot : slot + 1], (16, own)).astype(bf16)
            wanted = jnp.concatenate([wanted] * (count // 16), axis=0)
            chosen.append(jnp.where(row_ids == wanted, ones, zeros))
        rows.append(dot(table, jnp.concatenate(chosen, axis=1), ((1,), (0,))))
    for slot in range(slots):
        lanes = slice(slot % 2 * own, (slot % 2 + 1) * own)
        total = total + rows[slot // 2][:, lanes] * filters_ref[slot]
    return total


def inner_kernel(features_ref, x_minus_ref, x_plus_ref, neighbours_ref, filters_ref, total_ref, table_ref):
    parts = (features_ref, x_minus_ref, x_plus_ref)
    total_ref[...] = neighbour_sum(
        parts, 0, neighbours_ref, filters_ref, table_ref, jnp.zeros(total_ref.shape, f32)
    )


def outer_kernel(
    first, y_minus_ref, y_plus_ref, neighbours_ref, filters_ref, total_ref, features_ref, w_update_ref,
    result_ref, table_ref,
):
    parts = (y_minus_ref, y_plus_ref)
    total = neighbour_sum(parts, first, neighbours_ref, filters_ref, table_ref, total_ref[...])
    update = dot(total.T.astype(bf16), w_update_ref[...], ((1,), (0,)))
    result_ref[...] = features_ref[...].astype(f32) + update


def final_kernel(channels, base_ref, summed_ref, w_long_ref, updated_ref, forces_ref):
    summed = jnp.sum(summed_ref[...].astype(f32), axis=0)
    potentials = summed[:channels].T
    long_range = dot(potentials, w_long_ref[...], ((1,), (0,)), lax.Precision.HIGHEST)
    updated_ref[...] = (base_ref[...] + long_range).astype(bf16)
    forces_ref[...] = summed[channels : channels + 3]


def per_device(
    features, positions, wave_vectors, filter_width, w_charge, w_filter_in, filter_output_weight,
    update_weight, w_long, send_along_x, send_along_y, neighbours, neighbour_count, distances,
):
    own, width = features.shape
    channels = w_charge.shape[1]
    devices = lax.axis_size("gx") * lax.axis_size("gy")
    count = wave_vectors.shape[1] // devices
    ghosts = send_along_x.shape[1]
    struct = jax.ShapeDtypeStruct
    small = pltpu.CompilerParams(vmem_limit_bytes=24 * 1024 * 1024)

    copies, x_minus, x_plus = pl.pallas_call(
        send_kernel,
        out_shape=(
            struct((devices, payload_rows, own), bf16), struct((ghosts, width), bf16), struct((ghosts, width), bf16),
        ),
        in_specs=[pl.BlockSpec(memory_space=pltpu.HBM)] * 4,
        scratch_shapes=[
            pltpu.VMEM((own, width), bf16),
            pltpu.VMEM((3, own), f32),
            pltpu.VMEM((channels, width), bf16),
            pltpu.VMEM(send_along_x.shape, jnp.int32),
            pltpu.VMEM((payload_rows, own), f32),
            pltpu.SemaphoreType.DMA((4,)),
        ],
        compiler_params=small,
        name="send",
    )(*[
        pltpu.with_memory_space_constraint(array, pltpu.HBM)
        for array in (features, positions, w_charge.T, send_along_x)
    ])

    x_minus = passed_along(x_minus, "gx", 1)
    x_plus = passed_along(x_plus, "gx", -1)
    integers, factors = pl.pallas_call(
        lambda *refs: factors_kernel(channels, *refs),
        out_shape=(struct((count, payload_rows), bf16), struct((4 * channels, count), f32)),
        in_specs=[pl.BlockSpec(memory_space=pltpu.HBM)] * 2,
        scratch_shapes=[
            pltpu.VMEM((wave_vectors.shape[0], max(count, 128)), jnp.int32),
            pltpu.VMEM((1, channels), f32),
            pltpu.SemaphoreType.DMA((2,)),
        ],
        compiler_params=small,
        name="factors",
    )(*[pltpu.with_memory_space_constraint(array, pltpu.HBM) for array in (wave_vectors, filter_width[None, :])])

    later = (
        features, send_along_y, neighbours, neighbour_count[None, :], distances,
        w_filter_in, filter_output_weight, update_weight, w_long,
    )
    later = pl.pallas_call(
        hold_kernel,
        out_shape=tuple(struct(array.shape, array.dtype) for array in later),
        in_specs=[pl.BlockSpec(memory_space=pltpu.HBM)] * len(later),
        scratch_shapes=[pltpu.SemaphoreType.DMA((len(later),))],
        compiler_params=small,
        name="hold",
    )(*[pltpu.with_memory_space_constraint(array, pltpu.HBM) for array in later])
    y_minus, y_plus = pl.pallas_call(
        second_send_kernel,
        out_shape=(struct((ghosts, width), bf16), struct((ghosts, width), bf16)),
        compiler_params=small,
        name="second_send",
    )(later[0], x_minus, x_plus, later[1])
    gathered, x_minus, x_plus, y_minus, y_plus, integers, factors, later = lax.optimization_barrier(
        (over_devices(copies), x_minus, x_plus, y_minus, y_plus, integers, factors, later)
    )
    (
        features, _, neighbours, neighbour_count, distances,
        w_filter_in, filter_output_weight, update_weight, w_long,
    ) = later
    held_bytes = devices * own * (8 * count + 2 * (128 + 2 * payload_rows + result_rows))
    partial = pl.pallas_call(
        lambda *refs: waves_kernel(channels, *refs),
        out_shape=struct((devices, result_rows, own), bf16),
        scratch_shapes=[
            pltpu.VMEM((2 * count, devices * own), bf16),
            pltpu.VMEM((2, 4 * channels, count), bf16),
            pltpu.VMEM((payload_rows, devices * own), bf16),
            pltpu.VMEM((128, devices * own), bf16),
            pltpu.VMEM((count, devices * own), f32),
        ],
        compiler_params=pltpu.CompilerParams(vmem_limit_bytes=held_bytes + 8 * 1024 * 1024),
        cost_estimate=pl.CostEstimate(flops=40 * count * devices * own, bytes_accessed=1 << 20, transcendentals=0),
        name="waves",
    )(gathered, integers, factors)
    partial, x_minus, y_minus, y_plus = lax.optimization_barrier((partial, x_minus, y_minus, y_plus))
    received = over_devices(partial)

    y_minus = passed_along(y_minus, "gy", 1)
    y_plus = passed_along(y_plus, "gy", -1)
    slots = neighbours.shape[0]
    distances, w_filter_in, x_minus = lax.optimization_barrier((distances, w_filter_in, x_minus))
    filters = pl.pallas_call(
        filters_kernel,
        out_shape=struct((slots, width, own), f32),
        scratch_shapes=[pltpu.VMEM((32, width), f32), pltpu.VMEM(distances.shape, f32)],
        compiler_params=small,
        cost_estimate=pl.CostEstimate(
            flops=2 * slots * own * width * width, bytes_accessed=1 << 20, transcendentals=2 * slots * own * width
        ),
        name="filters",
    )(neighbour_count, distances, w_filter_in, filter_output_weight)
    inner_rows = own + 2 * ghosts
    inner = pl.pallas_call(
        inner_kernel,
        out_shape=struct((width, own), f32),
        scratch_shapes=[pltpu.VMEM((inner_rows, width), f32)],
        compiler_params=small,
        cost_estimate=pl.CostEstimate(
            flops=2 * slots * own * width * inner_rows, bytes_accessed=1 << 20, transcendentals=0
        ),
        name="inner",
    )(features, x_minus, x_plus, neighbours, filters)
    inner, y_minus, y_plus = lax.optimization_barrier((inner, y_minus, y_plus))
    base = pl.pallas_call(
        lambda *refs: outer_kernel(inner_rows, *refs),
        out_shape=struct((own, width), f32),
        scratch_shapes=[pltpu.VMEM((2 * ghosts, width), f32)],
        compiler_params=small,
        cost_estimate=pl.CostEstimate(
            flops=4 * slots * own * width * ghosts, bytes_accessed=1 << 20, transcendentals=0
        ),
        name="outer",
    )(y_minus, y_plus, neighbours, filters, inner, features, update_weight)

    updated, forces = pl.pallas_call(
        lambda *refs: final_kernel(channels, *refs),
        out_shape=(struct((own, width), bf16), struct((3, own), f32)),
        compiler_params=small,
        name="final",
    )(base, received, w_long)
    return updated, forces


def solution(mesh):
    placed = (
        P(("gx", "gy"), None),
        P(None, ("gx", "gy")),
        P(),
        P(),
        P(),
        P(),
        P(),
        P(),
        P(),
        P(None, ("gx", "gy")),
        P(None, ("gx", "gy")),
        P(None, ("gx", "gy")),
        P(("gx", "gy")),
        P(None, ("gx", "gy")),
    )
    return jax.shard_map(
        per_device,
        mesh=mesh,
        in_specs=placed,
        out_specs=(P(("gx", "gy"), None), P(None, ("gx", "gy"))),
        check_vma=False,
    )
```

```python
import math

import jax
import jax.numpy as jnp
from jax import lax
from jax.experimental import pallas as pl
from jax.experimental.pallas import tpu as pltpu
from jax.sharding import PartitionSpec as P

two_pi = 2.0 * math.pi
force_unit = 0.001
f32 = jnp.float32
bf16 = jnp.bfloat16

sin_terms = (4.442867902992535, -7.307443419719773, 3.594788063370906, -0.7843739903522723)
cos_terms = (1.414204080647301, -6.977642060724434, 5.715238411759286, -1.7283486673792663)

cos_scale = sin_terms[3] * sin_terms[3]
sin_scale = sin_terms[3] * cos_terms[3]

rounder = 1.5 * 2.0**23

payload_rows = 24
part_rows = ((0, 3), (3, 3), (6, 2))
result_rows = 24


def dot(a, b, contract, precision=None):
    return lax.dot_general(
        a, b, (contract, ((), ())), preferred_element_type=f32, precision=precision
    )


def passed_along(block, axis, distance):
    devices = range(lax.axis_size(axis))
    route = [((i - distance) % len(devices), i) for i in devices]
    return lax.ppermute(block, axis, route)


def place():
    return lax.axis_index("gx") * lax.axis_size("gy") + lax.axis_index("gy")


def over_devices(blocks):
    return lax.all_to_all(blocks, ("gx", "gy"), 0, 0, tiled=True)


def waves_of(turns):
    part = turns - ((turns + rounder) - rounder)
    square = part * part
    sine = part * polynomial(sin_terms, square)
    cosine = polynomial(cos_terms, square)
    return 1.0 / cos_scale - sine * sine, sine * cosine


def polynomial(terms, square):
    value = square + terms[2] / terms[3]
    for term in terms[1::-1]:
        value = value * square + term / terms[3]
    return value


def picked(list_row, tables):
    total, first = None, 0
    for table in tables:
        rows = table.shape[0]
        ids = lax.broadcasted_iota(jnp.int32, (rows, list_row.shape[1]), 0) + first
        chosen = jnp.where(ids == list_row, 1.0, 0.0).astype(bf16)
        part = dot(chosen, table, ((0,), (0,)))
        total = part if total is None else total + part
        first += rows
    return total


def fetched(given, held, semaphores):
    moves = [
        pltpu.make_async_copy(source, target, semaphores.at[i]) for i, (source, target) in enumerate(zip(given, held))
    ]
    for move in moves:
        move.start()
    for move in moves:
        move.wait()


def hold_kernel(*refs):
    count = (len(refs) - 1) // 2
    fetched(refs[:count], refs[count:-1], refs[-1])


def send_kernel(*refs):
    given, (copies_ref, minus_ref, plus_ref) = refs[:4], refs[4:7]
    held, rows_ref, semaphores = refs[7:11], refs[11], refs[12]
    fetched(given, held, semaphores)
    features_ref, positions_ref, w_charge_ref, lists_ref = held
    features = features_ref[...]
    channels = w_charge_ref.shape[0]
    charges = dot(w_charge_ref[...], features, ((1,), (1,))).astype(bf16).astype(f32)
    rows_ref[...] = jnp.zeros_like(rows_ref)
    rows_ref[0:channels, :] = charges
    left = positions_ref[...]
    for first, rows in part_rows:
        rounded = left.astype(bf16).astype(f32)
        rows_ref[channels + first : channels + first + rows, :] = rounded[:rows]
        left = left - rounded
    block = rows_ref[...].astype(bf16)

    def place(index, unused):
        copies_ref[index] = block
        return unused

    lax.fori_loop(0, copies_ref.shape[0], place, 0, unroll=8)
    minus_ref[...] = picked(lists_ref[0:1, :], [features]).astype(bf16)
    plus_ref[...] = picked(lists_ref[1:2, :], [features]).astype(bf16)


def second_send_kernel(features_ref, from_minus_ref, from_plus_ref, lists_ref, minus_ref, plus_ref):
    tables = [features_ref[...], from_minus_ref[...], from_plus_ref[...]]
    for direction, result_ref in enumerate((minus_ref, plus_ref)):
        result_ref[...] = picked(lists_ref[direction : direction + 1, :], tables).astype(bf16)


def factors_kernel(channels, vectors_ref, width_ref, integers_ref, factors_ref, held_ref, held_width_ref, semaphores):
    count = integers_ref.shape[0]
    window = held_ref.shape[1]
    offset = place() * count
    first = pl.multiple_of(offset // window * window, window)
    fetched((vectors_ref.at[:, pl.ds(first, window)], width_ref), (held_ref, held_width_ref), semaphores)
    vectors = held_ref[...].astype(f32)
    if window > count:
        vectors = pltpu.roll(vectors, lax.rem(window - (offset - first), window), 1)[:, :count]
    kx, ky, kz = vectors[0:1], vectors[1:2], vectors[2:3]
    squared = two_pi * two_pi * (kx * kx + ky * ky + 0.25 * kz * kz)
    diagonal = lax.broadcasted_iota(jnp.int32, (channels, channels), 0) == lax.broadcasted_iota(
        jnp.int32, (channels, channels), 1
    )
    width = jnp.sum(jnp.where(diagonal, held_width_ref[...], 0.0), axis=1, keepdims=True)
    weight = jnp.exp(-0.5 * (width * width) * squared) * (two_pi * two_pi / squared)
    factors_ref[...] = jnp.concatenate([weight] + [two_pi * along * weight for along in (kx, ky, kz)], axis=0)
    component = lax.broadcasted_iota(jnp.int32, (payload_rows, count), 0) - channels
    inside = (component >= 0) & (component < 8)
    component = lax.rem(jnp.maximum(component, 0), 3)
    integers = jnp.where(component == 0, kx, jnp.where(component == 1, ky, kz))
    integers_ref[...] = jnp.where(inside, integers, 0.0).T.astype(bf16)


per_tile = 4


def tile_of(blocks_ref, index):
    return jnp.concatenate([blocks_ref[per_tile * index + i] for i in range(per_tile)], axis=1)


def add_waves(channels, blocks_ref, integers_ref, waves_ref, joined_ref, weights_ref, turns_ref):
    devices, rows, own = blocks_ref.shape
    count = integers_ref.shape[0]
    chunk = min(count, 128)
    weights_ref[channels : 2 * channels, :] = jnp.ones((channels, devices * own), bf16)

    def join(index, unused):
        lanes = pl.ds(pl.multiple_of(index * own, own), own)
        block = blocks_ref[index]
        joined_ref[:, lanes] = block
        weights_ref[0:channels, lanes] = block[:channels]
        return unused

    lax.fori_loop(0, devices, join, 0, unroll=8)
    turns_ref[...] = dot(integers_ref[...], joined_ref[...], ((1,), (0,)))

    def step(index, unused):
        for part in range(8):
            lanes = pl.ds(pl.multiple_of((8 * index + part) * own, own), own)
            for first in range(0, count, chunk):
                cosine, sine = waves_of(turns_ref[first : first + chunk, lanes])
                waves_ref[first : first + chunk, lanes] = cosine.astype(bf16)
                waves_ref[count + first : count + first + chunk, lanes] = sine.astype(bf16)
        return unused

    lax.fori_loop(0, devices // 8, step, 0)
    sums = dot(waves_ref[...], weights_ref[...], ((1,), (1,)))
    return [sums[:count], sums[count:]]


def put_fields(channels, atoms, blocks_ref, waves_ref, coefficients_ref, mean, result_ref):
    devices, _, own = blocks_ref.shape
    count = coefficients_ref.shape[2]
    wide = per_tile * own
    scale = 1.0 / math.sqrt(atoms)

    def waves_at(index, wave):
        lanes = pl.ds(pl.multiple_of(index * wide, wide), wide)
        return waves_ref[wave * count : (wave + 1) * count, lanes]

    def step(turn, unused):
        indices = [4 * turn + i for i in range(4)]
        fields_of = [
            sum(dot(coefficients_ref[wave], waves_at(index, wave), ((1,), (0,))) for wave in range(2))
            for index in indices
        ]
        for index, fields in zip(indices, fields_of):
            fields = fields * scale
            centred = tile_of(blocks_ref, index)[:channels].astype(f32) - mean
            rows = [fields[:channels]]
            for axis in range(3):
                along = fields[(axis + 1) * channels : (axis + 2) * channels]
                rows.append(-force_unit * jnp.sum(centred * along, axis=0, keepdims=True))
            rows.append(jnp.zeros((result_rows - channels - 3, wide), f32))
            result = jnp.concatenate(rows, axis=0)
            for i in range(per_tile):
                result_ref[per_tile * index + i] = result[:, i * own : (i + 1) * own].astype(result_ref.dtype)
        return unused

    lax.fori_loop(0, devices // (4 * per_tile), step, 0)


def waves_kernel(channels, gathered_ref, integers_ref, factors_ref, result_ref, waves_ref, coefficients_ref, *scratch):
    devices, _, own = gathered_ref.shape
    atoms = devices * own
    sums = [total.T for total in add_waves(channels, gathered_ref, integers_ref, waves_ref, *scratch)]

    def add_up(index, total):
        return total + gathered_ref[index][:channels].astype(f32)

    total = lax.fori_loop(0, devices, add_up, jnp.zeros((channels, own), f32), unroll=8)
    mean = jnp.sum(total, axis=1, keepdims=True) * (1.0 / atoms)
    cosine, sine = [total[0:channels, :] - mean * total[channels : channels + 1, :] for total in sums]
    cosine, sine = cosine * cos_scale, sine * sin_scale
    factors = factors_ref[...]
    coefficients_ref[0] = (cos_scale * factors * jnp.concatenate([cosine] + [sine] * 3, axis=0)).astype(bf16)
    coefficients_ref[1] = (sin_scale * factors * jnp.concatenate([sine] + [-cosine] * 3, axis=0)).astype(bf16)
    put_fields(channels, atoms, gathered_ref, waves_ref, coefficients_ref, mean, result_ref)


filter_group = 32


def filters_kernel(count_ref, distances_ref, w_in_ref, w_out_ref, filters_ref, radial_ref, envelope_ref):
    slots, own = distances_ref.shape
    radial = w_in_ref.shape[0]
    radial_ref[...] = jnp.zeros_like(radial_ref)
    radial_ref[0:radial, :] = w_in_ref[...].astype(f32)
    w_in = radial_ref[...].T.astype(bf16)
    w_out = w_out_ref[...].astype(f32).T.astype(bf16)
    padded = radial_ref.shape[0]
    centers = 5.0 * lax.broadcasted_iota(jnp.int32, (padded, own), 0).astype(f32) / (radial - 1)
    sharpness = 0.02 * (radial - 1) * (radial - 1)
    live = lax.broadcasted_iota(jnp.int32, (slots, own), 0) < count_ref[...]
    envelope_ref[...] = jnp.where(live, 0.5 * (cos_scale * waves_of(0.1 * distances_ref[...])[0] + 1.0), 0.0)
    pairs = range(0, filter_group, 2)

    def step(turn, unused):
        start = pl.multiple_of(turn * filter_group, filter_group)
        lengths = distances_ref[pl.ds(start, filter_group), :]
        envelope = envelope_ref[pl.ds(start, filter_group), :]
        values, filters = [], []
        for pair in pairs:
            basis = []
            for slot in (pair, pair + 1):
                offsets = lengths[slot : slot + 1] - centers
                basis.append(jnp.exp(-sharpness * offsets * offsets).astype(bf16))
            values.append(dot(w_in, jnp.concatenate(basis, axis=1), ((1,), (0,))))
        for value in values:
            hidden = (jnp.log(1.0 + jnp.exp(value)) - math.log(2.0)).astype(bf16)
            filters.append(dot(w_out, hidden, ((1,), (0,))))
        for slot in range(filter_group):
            lanes = slice(slot % 2 * own, (slot % 2 + 1) * own)
            filters_ref[start + slot] = envelope[slot : slot + 1] * filters[slot // 2][:, lanes]
        return unused

    lax.fori_loop(0, slots // filter_group, step, 0)


def neighbour_sum(parts, first, neighbours_ref, filters_ref, table_ref, total):
    slots, own = neighbours_ref.shape
    count = table_ref.shape[0]
    filled = 0
    for part in parts:
        table_ref[filled : filled + part.shape[0], :] = part[...].astype(f32)
        filled += part.shape[0]
    table = table_ref[...].T.astype(bf16)
    row_ids = (lax.broadcasted_iota(jnp.int32, (count, own), 0) + first).astype(f32).astype(bf16)
    ones, zeros = jnp.ones((count, own), bf16), jnp.zeros((count, own), bf16)
    ids = neighbours_ref[...].astype(f32)
    rows = []
    for pair in range(0, slots, 2):
        chosen = []
        for slot in (pair, pair + 1):
            wanted = jnp.broadcast_to(ids[slot : slot + 1], (16, own)).astype(bf16)
            wanted = jnp.concatenate([wanted] * (count // 16), axis=0)
            chosen.append(jnp.where(row_ids == wanted, ones, zeros))
        rows.append(dot(table, jnp.concatenate(chosen, axis=1), ((1,), (0,))))
    for slot in range(slots):
        lanes = slice(slot % 2 * own, (slot % 2 + 1) * own)
        total = total + rows[slot // 2][:, lanes] * filters_ref[slot]
    return total


def inner_kernel(features_ref, x_minus_ref, x_plus_ref, neighbours_ref, filters_ref, total_ref, table_ref):
    parts = (features_ref, x_minus_ref, x_plus_ref)
    total_ref[...] = neighbour_sum(
        parts, 0, neighbours_ref, filters_ref, table_ref, jnp.zeros(total_ref.shape, f32)
    )


def outer_kernel(
    first, y_minus_ref, y_plus_ref, neighbours_ref, filters_ref, total_ref, features_ref, w_update_ref,
    result_ref, table_ref,
):
    parts = (y_minus_ref, y_plus_ref)
    total = neighbour_sum(parts, first, neighbours_ref, filters_ref, table_ref, total_ref[...])
    update = dot(total.T.astype(bf16), w_update_ref[...], ((1,), (0,)))
    result_ref[...] = features_ref[...].astype(f32) + update


def final_kernel(channels, base_ref, summed_ref, w_long_ref, updated_ref, forces_ref):
    summed = jnp.sum(summed_ref[...].astype(f32), axis=0)
    potentials = summed[:channels].T
    long_range = dot(potentials, w_long_ref[...], ((1,), (0,)), lax.Precision.HIGHEST)
    updated_ref[...] = (base_ref[...] + long_range).astype(bf16)
    forces_ref[...] = summed[channels : channels + 3]


def per_device(
    features, positions, wave_vectors, filter_width, w_charge, w_filter_in, filter_output_weight,
    update_weight, w_long, send_along_x, send_along_y, neighbours, neighbour_count, distances,
):
    own, width = features.shape
    channels = w_charge.shape[1]
    devices = lax.axis_size("gx") * lax.axis_size("gy")
    count = wave_vectors.shape[1] // devices
    ghosts = send_along_x.shape[1]
    struct = jax.ShapeDtypeStruct
    small = pltpu.CompilerParams(vmem_limit_bytes=24 * 1024 * 1024)

    copies, x_minus, x_plus = pl.pallas_call(
        send_kernel,
        out_shape=(
            struct((devices, payload_rows, own), bf16), struct((ghosts, width), bf16), struct((ghosts, width), bf16),
        ),
        in_specs=[pl.BlockSpec(memory_space=pltpu.HBM)] * 4,
        scratch_shapes=[
            pltpu.VMEM((own, width), bf16),
            pltpu.VMEM((3, own), f32),
            pltpu.VMEM((channels, width), bf16),
            pltpu.VMEM(send_along_x.shape, jnp.int32),
            pltpu.VMEM((payload_rows, own), f32),
            pltpu.SemaphoreType.DMA((4,)),
        ],
        compiler_params=small,
        name="send",
    )(*[
        pltpu.with_memory_space_constraint(array, pltpu.HBM)
        for array in (features, positions, w_charge.T, send_along_x)
    ])

    x_minus = passed_along(x_minus, "gx", 1)
    x_plus = passed_along(x_plus, "gx", -1)
    integers, factors = pl.pallas_call(
        lambda *refs: factors_kernel(channels, *refs),
        out_shape=(struct((count, payload_rows), bf16), struct((4 * channels, count), f32)),
        in_specs=[pl.BlockSpec(memory_space=pltpu.HBM)] * 2,
        scratch_shapes=[
            pltpu.VMEM((wave_vectors.shape[0], max(count, 128)), jnp.int32),
            pltpu.VMEM((1, channels), f32),
            pltpu.SemaphoreType.DMA((2,)),
        ],
        compiler_params=small,
        name="factors",
    )(*[pltpu.with_memory_space_constraint(array, pltpu.HBM) for array in (wave_vectors, filter_width[None, :])])

    later = (
        features, send_along_y, neighbours, neighbour_count[None, :], distances,
        w_filter_in, filter_output_weight, update_weight, w_long,
    )
    later = pl.pallas_call(
        hold_kernel,
        out_shape=tuple(struct(array.shape, array.dtype) for array in later),
        in_specs=[pl.BlockSpec(memory_space=pltpu.HBM)] * len(later),
        scratch_shapes=[pltpu.SemaphoreType.DMA((len(later),))],
        compiler_params=small,
        name="hold",
    )(*[pltpu.with_memory_space_constraint(array, pltpu.HBM) for array in later])
    y_minus, y_plus = pl.pallas_call(
        second_send_kernel,
        out_shape=(struct((ghosts, width), bf16), struct((ghosts, width), bf16)),
        compiler_params=small,
        name="second_send",
    )(later[0], x_minus, x_plus, later[1])
    gathered, x_minus, x_plus, y_minus, y_plus, integers, factors, later = lax.optimization_barrier(
        (over_devices(copies), x_minus, x_plus, y_minus, y_plus, integers, factors, later)
    )
    (
        features, _, neighbours, neighbour_count, distances,
        w_filter_in, filter_output_weight, update_weight, w_long,
    ) = later
    held_bytes = devices * own * (8 * count + 2 * (2 * channels + 2 * payload_rows + result_rows))
    partial = pl.pallas_call(
        lambda *refs: waves_kernel(channels, *refs),
        out_shape=struct((devices, result_rows, own), bf16),
        scratch_shapes=[
            pltpu.VMEM((2 * count, devices * own), bf16),
            pltpu.VMEM((2, 4 * channels, count), bf16),
            pltpu.VMEM((payload_rows, devices * own), bf16),
            pltpu.VMEM((2 * channels, devices * own), bf16),
            pltpu.VMEM((count, devices * own), f32),
        ],
        compiler_params=pltpu.CompilerParams(vmem_limit_bytes=held_bytes + 8 * 1024 * 1024),
        cost_estimate=pl.CostEstimate(flops=40 * count * devices * own, bytes_accessed=1 << 20, transcendentals=0),
        name="waves",
    )(gathered, integers, factors)
    partial, x_minus, y_minus, y_plus = lax.optimization_barrier((partial, x_minus, y_minus, y_plus))
    received = over_devices(partial)

    y_minus = passed_along(y_minus, "gy", 1)
    y_plus = passed_along(y_plus, "gy", -1)
    slots = neighbours.shape[0]
    distances, w_filter_in, x_minus = lax.optimization_barrier((distances, w_filter_in, x_minus))
    filters = pl.pallas_call(
        filters_kernel,
        out_shape=struct((slots, width, own), f32),
        scratch_shapes=[pltpu.VMEM((32, width), f32), pltpu.VMEM(distances.shape, f32)],
        compiler_params=small,
        cost_estimate=pl.CostEstimate(
            flops=2 * slots * own * width * width, bytes_accessed=1 << 20, transcendentals=2 * slots * own * width
        ),
        name="filters",
    )(neighbour_count, distances, w_filter_in, filter_output_weight)
    inner_rows = own + 2 * ghosts
    inner = pl.pallas_call(
        inner_kernel,
        out_shape=struct((width, own), f32),
        scratch_shapes=[pltpu.VMEM((inner_rows, width), f32)],
        compiler_params=small,
        cost_estimate=pl.CostEstimate(
            flops=2 * slots * own * width * inner_rows, bytes_accessed=1 << 20, transcendentals=0
        ),
        name="inner",
    )(features, x_minus, x_plus, neighbours, filters)
    inner, y_minus, y_plus = lax.optimization_barrier((inner, y_minus, y_plus))
    base = pl.pallas_call(
        lambda *refs: outer_kernel(inner_rows, *refs),
        out_shape=struct((own, width), f32),
        scratch_shapes=[pltpu.VMEM((2 * ghosts, width), f32)],
        compiler_params=small,
        cost_estimate=pl.CostEstimate(
            flops=4 * slots * own * width * ghosts, bytes_accessed=1 << 20, transcendentals=0
        ),
        name="outer",
    )(y_minus, y_plus, neighbours, filters, inner, features, update_weight)

    updated, forces = pl.pallas_call(
        lambda *refs: final_kernel(channels, *refs),
        out_shape=(struct((own, width), bf16), struct((3, own), f32)),
        compiler_params=small,
        name="final",
    )(base, received, w_long)
    return updated, forces


def solution(mesh):
    placed = (
        P(("gx", "gy"), None),
        P(None, ("gx", "gy")),
        P(),
        P(),
        P(),
        P(),
        P(),
        P(),
        P(),
        P(None, ("gx", "gy")),
        P(None, ("gx", "gy")),
        P(None, ("gx", "gy")),
        P(("gx", "gy")),
        P(None, ("gx", "gy")),
    )
    return jax.shard_map(
        per_device,
        mesh=mesh,
        in_specs=placed,
        out_specs=(P(("gx", "gy"), None), P(None, ("gx", "gy"))),
        check_vma=False,
    )
```
